32 devices in a mesh: dp: 4 (over y, core), seq: 8 (over z, x).
Axes of the slice: x: 2, y: 2, z: 4, core: 2. Of those that a mesh axis runs over, the one named last changes fastest.
Arguments:
- inputs: bfloat16 [2, 65536, 2048], P(None, 'seq', 'dp'), may hold values from -6 to 6
- cotangent: bfloat16 [2, 65536, 2048], P(None, 'seq', 'dp'), may hold values from -6 to 6
- kernel: bfloat16 [65536, 2048], P('seq', 'dp'), may hold values from -6 to 6
- factor_one: bfloat16 [256, 256], replicated, may hold values from -0.375 to 0.375
- factor_two: bfloat16 [256, 256], replicated, may hold values from -0.375 to 0.375
Outputs:
- grad_inputs: bfloat16 [2, 65536, 2048], P(None, 'seq', 'dp')
- grad_kernel: bfloat16 [65536, 2048], P('seq', 'dp')
- grad_factor_one: float32 [256, 256], replicated
- grad_factor_two: float32 [256, 256], replicated
The draws below stay inside these ranges and needn't reach their ends.
All inputs are finite; a program needn't handle non-finite values.
Results may differ from the reference program's by a relative error of at most 0.0085.
Values may be sent and summed in bfloat16 or wider, within the bound.
No kernel may reach another device: no remote copies, remote signals or barrier semaphores. Data moves between devices by JAX's collectives and lax.ppermute only.
A program may use at most 256 MiB of HBM per device.

```python
import math
import jax
import jax.numpy as jnp
from jax import lax

D = 2048
BLOCK = 256
NB = 256
BATCH = 2
SEQ_LEN = 65536


def block_scale(stream_key, extent, split, smallest, high):
    def one(axis_at, blocks):
        steps = jax.random.uniform(jax.random.fold_in(jax.random.fold_in(stream_key, 6), axis_at), (blocks,), jnp.float32, smallest / len(split), high / len(split))
        return jnp.repeat(jnp.exp(steps), extent[axis_at] // blocks).reshape((-1,) + (1,) * (len(extent) - axis_at - 1))

    gain = one(*split[0])
    for cut in split[1:]:
        gain = gain * one(*cut)
    return gain


def normal_values(own_key, shape, spread, limit, pieces=(), kind=jnp.bfloat16):
    drawn = spread * jax.random.normal(own_key, shape, jnp.float32)
    if pieces:
        drawn = drawn * block_scale(own_key, shape, pieces, -0.22, 0.18)
    return jnp.clip(drawn, -limit, limit).astype(kind)


def setup_inputs(seed: int = 0) -> dict:
    streams_of = jax.random.split(jax.random.key(seed), 6)
    inputs = normal_values(streams_of[0], (BATCH, SEQ_LEN, D), 1.0, 6.0, ((1, 8), (2, 4)))
    cotangent = normal_values(streams_of[1], (BATCH, SEQ_LEN, D), 1.0, 6.0, ((1, 8), (2, 4)))
    kernel = normal_values(streams_of[2], (SEQ_LEN, D), 1.0, 6.0, ((0, 8), (1, 4)))
    factor_one = normal_values(streams_of[3], (BLOCK, BLOCK), BLOCK ** -0.5, 0.375)
    factor_two = normal_values(streams_of[4], (NB, NB), NB ** -0.5, 0.375)
    return dict(inputs=inputs, cotangent=cotangent, kernel=kernel, factor_one=factor_one, factor_two=factor_two)


def to_half(values):
    return lax.optimization_barrier(values.astype(jnp.bfloat16)).astype(jnp.float32)

def reference(inputs, cotangent, kernel, factor_one, factor_two):
    first_factor = factor_one.astype(jnp.float32)
    second_factor = factor_two.astype(jnp.float32)
    kernel_cube = kernel.astype(jnp.float32).reshape(NB, BLOCK, D)

    def sequence(totals, slices):
        grad_first, grad_second, kernel_total = totals
        inputs_seq = slices[0].astype(jnp.float32).reshape(NB, BLOCK, D)
        grads_seq = slices[1].astype(jnp.float32).reshape(NB, BLOCK, D)
        within_mix = to_half(jnp.einsum('cb,abh->ach', first_factor, inputs_seq))
        spectrum = to_half(jnp.einsum('ea,ach->ech', second_factor, within_mix))
        weighted = to_half(kernel_cube * spectrum)
        returned = to_half(jnp.einsum('ea,ech->ach', second_factor, weighted))
        grad_within = to_half(jnp.einsum('cb,abh->ach', first_factor, grads_seq))
        grad_spectrum = to_half(jnp.einsum('ea,ach->ech', second_factor, grad_within))
        grad_weighted = to_half(kernel_cube * grad_spectrum)
        grad_returned = to_half(jnp.einsum('ea,ech->ach', second_factor, grad_weighted))
        grad_seq = jnp.einsum('cb,ach->abh', first_factor, grad_returned).astype(jnp.bfloat16)
        kernel_total = kernel_total + grad_spectrum * spectrum
        grad_first = grad_first + jnp.einsum('ach,abh->cb', returned, grads_seq) + jnp.einsum('ach,abh->cb', grad_returned, inputs_seq)
        grad_second = grad_second + jnp.einsum('ach,ech->ea', grad_within, weighted) + jnp.einsum('ech,ach->ea', grad_weighted, within_mix)
        return ((grad_first, grad_second, kernel_total), grad_seq.reshape(SEQ_LEN, D))
    start = (jnp.zeros((BLOCK, BLOCK), jnp.float32), jnp.zeros((NB, NB), jnp.float32), jnp.zeros((NB, BLOCK, D), jnp.float32))
    totals, grad_inputs = lax.scan(sequence, start, (inputs, cotangent))
    grad_first, grad_second, kernel_total = totals
    scale_first = 1.0 / math.sqrt(BATCH * NB * D)
    scale_second = 1.0 / math.sqrt(BATCH * BLOCK * D)
    grad_kernel = kernel_total.reshape(SEQ_LEN, D).astype(jnp.bfloat16)
    return (grad_inputs, grad_kernel, grad_first * scale_first, grad_second * scale_second)
```

```python
import functools
import math

import jax
import jax.numpy as jnp
from jax import lax
from jax.experimental import pallas as pl
from jax.experimental.pallas import tpu as pltpu
from jax.sharding import PartitionSpec as P

WINDOW = 6
VMEM_BYTES = 60 * 1024 * 1024
LANES = 128
ROWS = 16


def matmul(left, right):
    return jnp.dot(left, right, preferred_element_type=jnp.float32)


def matmul_rows(left, right):
    return lax.dot_general(left, right, (((0,), (0,)), ((), ())), preferred_element_type=jnp.float32)


def matmul_columns(left, right):
    return lax.dot_general(left, right, (((1,), (1,)), ((), ())), preferred_element_type=jnp.float32)


def leave_kernel(group, me_ref, values_ref, *refs):
    outs, held = refs[:-1], refs[-1]
    mine = lax.rem(me_ref[0], group)
    turned = jnp.stack([values_ref[0, i].T for i in range(values_ref.shape[1])])
    held[...] = jnp.swapaxes(turned, 0, 1).reshape(held.shape)
    for j, out in enumerate(outs):
        out[...] = held[mine ^ j]


def leave(values, place, me, lane_block, group):
    _, blocks, width, channels = values.shape
    lanes = min(LANES, channels)
    own = lanes // group
    rows = math.gcd(blocks, ROWS)
    spec = pl.BlockSpec((own, rows, width), lambda i, me: (0, i, 0))
    return pl.pallas_call(
        functools.partial(leave_kernel, group),
        grid_spec=pltpu.PrefetchScalarGridSpec(
            num_scalar_prefetch=1,
            grid=(blocks // rows,),
            in_specs=[
                pl.BlockSpec((1, rows, width, lanes), lambda i, me: (place, i, 0, (me[0] // group) ^ lane_block))
            ],
            out_specs=[spec] * group,
            scratch_shapes=[pltpu.VMEM((group, own, rows, width), values.dtype)],
        ),
        out_shape=[jax.ShapeDtypeStruct((own, blocks, width), values.dtype)] * group,
        compiler_params=pltpu.CompilerParams(vmem_limit_bytes=VMEM_BYTES),
        cost_estimate=pl.CostEstimate(
            flops=0, bytes_accessed=4 * blocks * width * lanes, transcendentals=0
        ),
    )(me, values)


def arrive_kernel(group, me_ref, *refs):
    pieces, out_ref, held = refs[:group], refs[-2], refs[-1]
    own, blocks, width = pieces[0].shape
    mine = lax.rem(me_ref[0], group)
    for j, piece in enumerate(pieces):
        held[mine ^ j] = piece[...]
    turned = jnp.swapaxes(held[...].reshape(group * own, blocks, width), 0, 1)
    for i in range(blocks):
        out_ref[0, i] = turned[i].T


def arrive(pieces, me, lane_block, place, count, channels, onto):
    group = len(pieces)
    own, blocks, width = pieces[0].shape
    lanes = own * group
    rows = math.gcd(blocks, ROWS)
    spec = pl.BlockSpec((own, rows, width), lambda i, me: (0, i, 0))
    aliased = onto is not None
    return pl.pallas_call(
        functools.partial(arrive_kernel, group),
        grid_spec=pltpu.PrefetchScalarGridSpec(
            num_scalar_prefetch=1,
            grid=(blocks // rows,),
            in_specs=[spec] * group + ([pl.BlockSpec(memory_space=pl.ANY)] if aliased else []),
            out_specs=pl.BlockSpec(
                (1, rows, width, lanes), lambda i, me: (place, i, 0, (me[0] // group) ^ lane_block)
            ),
            scratch_shapes=[pltpu.VMEM((group, own, rows, width), pieces[0].dtype)],
        ),
        out_shape=jax.ShapeDtypeStruct((count, blocks, width, channels), pieces[0].dtype),
        input_output_aliases={group + 1: 0} if aliased else {},
        compiler_params=pltpu.CompilerParams(vmem_limit_bytes=VMEM_BYTES),
        cost_estimate=pl.CostEstimate(
            flops=0, bytes_accessed=4 * blocks * width * lanes, transcendentals=0
        ),
    )(me, *pieces, *((onto,) if aliased else ()))


def mix_kernel(parts, has_previous, is_last, *refs):
    refs = list(refs)
    take = lambda count: [refs.pop(0) for _ in range(count)]
    x_refs, y_refs, k_refs = take(parts), take(parts), take(parts)
    previous_ref = take(1)[0] if has_previous else None
    one_ref, one_t_ref, two_ref, two_t_ref = take(4)
    grad_refs = take(parts)
    kernel_refs = take(parts if is_last else 1)
    first_ref, second_ref = refs
    channel_count, part_rows, width = x_refs[0].shape

    @pl.when(pl.program_id(0) == 0)
    def _():
        first_ref[...] = jnp.zeros_like(first_ref)
        second_ref[...] = jnp.zeros_like(second_ref)

    def whole(group, channel):
        return jnp.concatenate([r[channel] for r in group], axis=0)

    def spread(group, channel, values):
        for part, ref in enumerate(group):
            ref[channel] = values[part * part_rows : (part + 1) * part_rows]

    one, one_t, two, two_t = one_ref[...], one_t_ref[...], two_ref[...], two_t_ref[...]
    first_sum = None
    second_sum = None
    for channel in range(channel_count):
        x, y = whole(x_refs, channel), whole(y_refs, channel)
        k = whole(k_refs, channel).astype(jnp.float32)
        a = matmul(x, one_t).astype(jnp.bfloat16)
        g = matmul(y, one_t).astype(jnp.bfloat16)
        s = matmul(two, a).astype(jnp.bfloat16).astype(jnp.float32)
        h = matmul(two, g).astype(jnp.bfloat16).astype(jnp.float32)
        z = (k * s).astype(jnp.bfloat16)
        w = (k * h).astype(jnp.bfloat16)
        kernel_terms = s * h
        if has_previous:
            kernel_terms = kernel_terms + previous_ref[channel]
        if is_last:
            spread(kernel_refs, channel, kernel_terms.astype(jnp.bfloat16))
        else:
            kernel_refs[0][channel] = kernel_terms
        c = matmul(two_t, z).astype(jnp.bfloat16)
        v = matmul(two_t, w).astype(jnp.bfloat16)
        spread(grad_refs, channel, matmul(v, one).astype(jnp.bfloat16))
        first = matmul_rows(c, y) + matmul_rows(v, x)
        second = matmul_columns(z, g) + matmul_columns(w, a)
        first_sum = first if first_sum is None else first_sum + first
        second_sum = second if second_sum is None else second_sum + second
    first_ref[...] += first_sum
    second_ref[...] += second_sum


def mix(x, y, k, previous, is_last, factors):
    parts = len(k)
    channels, part_rows, width = k[0].shape
    rows = parts * part_rows
    step = math.gcd(channels, 4)
    block = pl.BlockSpec((step, part_rows, width), lambda i: (i, 0, 0))
    tall = pl.BlockSpec((step, rows, width), lambda i: (i, 0, 0))
    has_previous = previous is not None
    small = [pl.BlockSpec(f.shape, lambda i: (0, 0)) for f in factors]
    sums = [jax.ShapeDtypeStruct((width, width), jnp.float32), jax.ShapeDtypeStruct((rows, rows), jnp.float32)]
    piece = jax.ShapeDtypeStruct((channels, part_rows, width), jnp.bfloat16)
    partial = jax.ShapeDtypeStruct((channels, rows, width), jnp.float32)
    out = pl.pallas_call(
        functools.partial(mix_kernel, parts, has_previous, is_last),
        grid=(channels // step,),
        in_specs=[block] * (3 * parts) + [tall] * has_previous + small,
        out_specs=[block] * parts
        + ([block] * parts if is_last else [tall])
        + [pl.BlockSpec(s.shape, lambda i: (0, 0)) for s in sums],
        out_shape=[piece] * parts + ([piece] * parts if is_last else [partial]) + sums,
        compiler_params=pltpu.CompilerParams(
            dimension_semantics=("arbitrary",), vmem_limit_bytes=VMEM_BYTES
        ),
        cost_estimate=pl.CostEstimate(
            flops=22 * channels * rows * width * width,
            bytes_accessed=12 * channels * rows * width,
            transcendentals=0,
        ),
    )(*x, *y, *k, *((previous,) if has_previous else ()), *factors)
    return out[:parts], out[parts:-2], out[-2], out[-1]


class Sends:
    def __init__(self, parts):
        self.parts = parts
        self.results = []

    def order(self):
        half = self.parts // 2
        far, near = list(range(half, self.parts)), list(range(1, half))
        mixed = []
        while far or near:
            mixed += [q.pop(0) for q in (far, near) if q]
        return mixed

    def __call__(self, pieces, hooks=(), first_window=WINDOW):
        places = {}
        hooked = []
        for step, k in enumerate(self.order()):
            values = pieces[k]
            for at, make in hooks:
                if at == step:
                    values, made = lax.optimization_barrier((values, make()))
                    hooked.append(made)
            window = min(WINDOW, first_window + step)
            if len(self.results) >= window:
                values, self.results[-window] = lax.optimization_barrier((values, self.results[-window]))
            pairs = [(i, i ^ k) for i in range(self.parts)]
            places[k] = len(self.results)
            self.results.append(lax.ppermute(values, "seq", pairs))
        return ((pieces[0], places), *hooked) if hooks else (pieces[0], places)

    def get(self, sent):
        own, places = sent
        return [own] + [self.results[places[k]] for k in range(1, self.parts)]


def on_device(inputs, cotangent, kernel, factor_one, factor_two):
    batch_count, row_count, channels = inputs.shape
    block_size = factor_one.shape[0]
    block_count = factor_two.shape[0]
    local_blocks = row_count // block_size
    parts = lax.axis_size("seq")
    own = channels // parts
    group = min(LANES, channels) // own
    me = lax.axis_index("seq")
    me_array = me.reshape(1).astype(jnp.int32)
    send = Sends(parts)

    def pack(values, place):
        cube = values.reshape(-1, local_blocks, block_size, channels)
        pieces = []
        for lane_block in range(parts // group):
            pieces += leave(cube, place, me_array, lane_block, group)
        return pieces

    def unpack(pieces, place, count, onto):
        for lane_block in range(parts // group):
            some = pieces[lane_block * group : (lane_block + 1) * group]
            onto = arrive(some, me_array, lane_block, place, count, channels, onto)
        return onto

    def relative(values, axis):
        starts = [(me ^ k) * local_blocks for k in range(parts)]
        return jnp.concatenate([lax.dynamic_slice_in_dim(values, s, local_blocks, axis) for s in starts], axis)

    two = relative(relative(factor_two, 0), 1)
    factors = (factor_one, factor_one.T, two, two.T)
    kernel_sent = send(pack(kernel, 0))
    batch_sent = [(send(pack(inputs, n)), send(pack(cotangent, n))) for n in range(batch_count)]
    k_all = send.get(kernel_sent)
    grads_sent = []
    previous = None
    first_sum = second_sum = 0.0
    for n, (x_sent, y_sent) in enumerate(batch_sent):
        is_last = n == batch_count - 1
        grads, kernel_grads, first, second = mix(send.get(x_sent), send.get(y_sent), k_all, previous, is_last, factors)
        previous = kernel_grads[0]
        first_sum, second_sum = first_sum + first, second_sum + second
        if not is_last:
            grads_sent.append(send(grads))

    axes = ("dp", "seq")
    devices = lax.axis_size(axes)

    def reduced():
        both = jnp.concatenate([first_sum, relative(relative(second_sum, 0), 1)])
        shares = both.reshape(devices, -1, both.shape[1])
        return jnp.sum(lax.all_to_all(shares, axes, 0, 0, tiled=True), axis=0)

    def early_grads():
        done = None
        for n, sent in enumerate(grads_sent):
            done = unpack(send.get(sent), n, batch_count, done)
        return done

    kernel_sent = send(kernel_grads, first_window=2)
    steps = parts - 1
    last_sent, share, grad_inputs, grad_kernel = send(
        grads,
        (
            (0, reduced),
            (steps // 2, early_grads),
            (steps - 1, lambda: unpack(send.get(kernel_sent), 0, 1, None)),
        ),
    )
    last = send.get(last_sent)
    share, last[-1] = lax.optimization_barrier((share, last[-1]))
    copies = jnp.broadcast_to(share, (devices, *share.shape))
    totals = lax.all_to_all(copies, axes, 0, 0, tiled=True).reshape(-1, block_size)
    first_total, second_total = totals[:block_size], totals[block_size:]
    grad_inputs = unpack(last, batch_count - 1, batch_count, grad_inputs)
    full_width = channels * lax.axis_size("dp")
    scale_first = 1.0 / math.sqrt(batch_count * block_count * full_width)
    scale_second = 1.0 / math.sqrt(batch_count * block_size * full_width)
    return (
        grad_inputs.reshape(inputs.shape),
        grad_kernel.reshape(kernel.shape),
        first_total * scale_first,
        second_total * scale_second,
    )


def solution(mesh):
    return jax.shard_map(
        on_device,
        mesh=mesh,
        in_specs=(P(None, "seq", "dp"), P(None, "seq", "dp"), P("seq", "dp"), P(), P()),
        out_specs=(P(None, "seq", "dp"), P("seq", "dp"), P(), P()),
        check_vma=False,
    )
```

```python
import functools
import math

import jax
import jax.numpy as jnp
from jax import lax
from jax.experimental import pallas as pl
from jax.experimental.pallas import tpu as pltpu
from jax.sharding import PartitionSpec as P

WINDOW = 6
VMEM_BYTES = 60 * 1024 * 1024
LANES = 128
ROWS = 16


def matmul(left, right):
    return jnp.dot(left, right, preferred_element_type=jnp.float32)


def matmul_rows(left, right):
    return lax.dot_general(left, right, (((0,), (0,)), ((), ())), preferred_element_type=jnp.float32)


def matmul_columns(left, right):
    return lax.dot_general(left, right, (((1,), (1,)), ((), ())), preferred_element_type=jnp.float32)


def leave_kernel(group, me_ref, values_ref, *refs):
    outs, held = refs[:-1], refs[-1]
    mine = lax.rem(me_ref[0], group)
    turned = jnp.stack([values_ref[0, i].T for i in range(values_ref.shape[1])])
    held[...] = jnp.swapaxes(turned, 0, 1).reshape(held.shape)
    for j, out in enumerate(outs):
        out[...] = held[mine ^ j]


def leave(values, place, me, lane_block, group):
    _, blocks, width, channels = values.shape
    lanes = min(LANES, channels)
    own = lanes // group
    rows = math.gcd(blocks, ROWS)
    spec = pl.BlockSpec((own, rows, width), lambda i, me: (0, i, 0))
    return pl.pallas_call(
        functools.partial(leave_kernel, group),
        grid_spec=pltpu.PrefetchScalarGridSpec(
            num_scalar_prefetch=1,
            grid=(blocks // rows,),
            in_specs=[
                pl.BlockSpec((1, rows, width, lanes), lambda i, me: (place, i, 0, (me[0] // group) ^ lane_block))
            ],
            out_specs=[spec] * group,
            scratch_shapes=[pltpu.VMEM((group, own, rows, width), values.dtype)],
        ),
        out_shape=[jax.ShapeDtypeStruct((own, blocks, width), values.dtype)] * group,
        compiler_params=pltpu.CompilerParams(vmem_limit_bytes=VMEM_BYTES),
        cost_estimate=pl.CostEstimate(
            flops=0, bytes_accessed=4 * blocks * width * lanes, transcendentals=0
        ),
    )(me, values)


def arrive_kernel(group, me_ref, *refs):
    pieces, out_ref, held = refs[:group], refs[-2], refs[-1]
    own, blocks, width = pieces[0].shape
    mine = lax.rem(me_ref[0], group)
    for j, piece in enumerate(pieces):
        held[mine ^ j] = piece[...]
    turned = jnp.swapaxes(held[...].reshape(group * own, blocks, width), 0, 1)
    for i in range(blocks):
        out_ref[0, i] = turned[i].T


def arrive(pieces, me, lane_block, place, count, channels, onto):
    group = len(pieces)
    own, blocks, width = pieces[0].shape
    lanes = own * group
    rows = math.gcd(blocks, ROWS)
    spec = pl.BlockSpec((own, rows, width), lambda i, me: (0, i, 0))
    aliased = onto is not None
    return pl.pallas_call(
        functools.partial(arrive_kernel, group),
        grid_spec=pltpu.PrefetchScalarGridSpec(
            num_scalar_prefetch=1,
            grid=(blocks // rows,),
            in_specs=[spec] * group + ([pl.BlockSpec(memory_space=pl.ANY)] if aliased else []),
            out_specs=pl.BlockSpec(
                (1, rows, width, lanes), lambda i, me: (place, i, 0, (me[0] // group) ^ lane_block)
            ),
            scratch_shapes=[pltpu.VMEM((group, own, rows, width), pieces[0].dtype)],
        ),
        out_shape=jax.ShapeDtypeStruct((count, blocks, width, channels), pieces[0].dtype),
        input_output_aliases={group + 1: 0} if aliased else {},
        compiler_params=pltpu.CompilerParams(vmem_limit_bytes=VMEM_BYTES),
        cost_estimate=pl.CostEstimate(
            flops=0, bytes_accessed=4 * blocks * width * lanes, transcendentals=0
        ),
    )(me, *pieces, *((onto,) if aliased else ()))


def mix_kernel(parts, has_previous, is_last, *refs):
    refs = list(refs)
    take = lambda count: [refs.pop(0) for _ in range(count)]
    x_refs, y_refs, k_refs = take(parts), take(parts), take(parts)
    previous_ref = take(1)[0] if has_previous else None
    one_ref, one_t_ref, two_ref, two_t_ref = take(4)
    grad_refs = take(parts)
    kernel_refs = take(parts if is_last else 1)
    first_ref, second_ref = refs
    channel_count, part_rows, width = x_refs[0].shape
    rows = parts * part_rows

    @pl.when(pl.program_id(0) == 0)
    def _():
        first_ref[...] = jnp.zeros_like(first_ref)
        second_ref[...] = jnp.zeros_like(second_ref)

    def whole(group, channel):
        return jnp.concatenate([r[channel] for r in group], axis=0)

    def spread(group, channel, values):
        for part, ref in enumerate(group):
            ref[channel] = values[part * part_rows : (part + 1) * part_rows]

    one, one_t, two, two_t = one_ref[...], one_t_ref[...], two_ref[...], two_t_ref[...]
    channels = range(channel_count)
    x = [whole(x_refs, channel) for channel in channels]
    y = [whole(y_refs, channel) for channel in channels]
    within = matmul(jnp.concatenate(x + y), one_t).astype(jnp.bfloat16)
    a = [within[i * rows : (i + 1) * rows] for i in channels]
    g = [within[(channel_count + i) * rows : (channel_count + i + 1) * rows] for i in channels]
    z, w, c, v = [], [], [], []
    for channel in channels:
        k = whole(k_refs, channel).astype(jnp.float32)
        s = matmul(two, a[channel]).astype(jnp.bfloat16).astype(jnp.float32)
        h = matmul(two, g[channel]).astype(jnp.bfloat16).astype(jnp.float32)
        z.append((k * s).astype(jnp.bfloat16))
        w.append((k * h).astype(jnp.bfloat16))
        kernel_terms = s * h
        if has_previous:
            kernel_terms = kernel_terms + previous_ref[channel]
        if is_last:
            spread(kernel_refs, channel, kernel_terms.astype(jnp.bfloat16))
        else:
            kernel_refs[0][channel] = kernel_terms
        c.append(matmul(two_t, z[channel]).astype(jnp.bfloat16))
        v.append(matmul(two_t, w[channel]).astype(jnp.bfloat16))
    grad = matmul(jnp.concatenate(v), one).astype(jnp.bfloat16)
    for channel in channels:
        spread(grad_refs, channel, grad[channel * rows : (channel + 1) * rows])
    first_ref[...] += matmul_rows(jnp.concatenate(c + v), jnp.concatenate(y + x))
    second_ref[...] += matmul_columns(jnp.concatenate(z + w, axis=1), jnp.concatenate(g + a, axis=1))


def mix(x, y, k, previous, is_last, factors):
    parts = len(k)
    channels, part_rows, width = k[0].shape
    rows = parts * part_rows
    step = math.gcd(channels, 4)
    block = pl.BlockSpec((step, part_rows, width), lambda i: (i, 0, 0))
    tall = pl.BlockSpec((step, rows, width), lambda i: (i, 0, 0))
    has_previous = previous is not None
    small = [pl.BlockSpec(f.shape, lambda i: (0, 0)) for f in factors]
    sums = [jax.ShapeDtypeStruct((width, width), jnp.float32), jax.ShapeDtypeStruct((rows, rows), jnp.float32)]
    piece = jax.ShapeDtypeStruct((channels, part_rows, width), jnp.bfloat16)
    partial = jax.ShapeDtypeStruct((channels, rows, width), jnp.float32)
    out = pl.pallas_call(
        functools.partial(mix_kernel, parts, has_previous, is_last),
        grid=(channels // step,),
        in_specs=[block] * (3 * parts) + [tall] * has_previous + small,
        out_specs=[block] * parts
        + ([block] * parts if is_last else [tall])
        + [pl.BlockSpec(s.shape, lambda i: (0, 0)) for s in sums],
        out_shape=[piece] * parts + ([piece] * parts if is_last else [partial]) + sums,
        compiler_params=pltpu.CompilerParams(
            dimension_semantics=("arbitrary",), vmem_limit_bytes=VMEM_BYTES
        ),
        cost_estimate=pl.CostEstimate(
            flops=22 * channels * rows * width * width,
            bytes_accessed=12 * channels * rows * width,
            transcendentals=0,
        ),
    )(*x, *y, *k, *((previous,) if has_previous else ()), *factors)
    return out[:parts], out[parts:-2], out[-2], out[-1]


class Sends:
    def __init__(self, parts):
        self.parts = parts
        self.results = []

    def order(self):
        half = self.parts // 2
        far, near = list(range(half, self.parts)), list(range(1, half))
        mixed = []
        while far or near:
            mixed += [q.pop(0) for q in (far, near) if q]
        return mixed

    def __call__(self, pieces, hooks=(), first_window=WINDOW):
        places = {}
        hooked = []
        for step, k in enumerate(self.order()):
            values = pieces[k]
            for at, make in hooks:
                if at == step:
                    values, made = lax.optimization_barrier((values, make()))
                    hooked.append(made)
            window = min(WINDOW, first_window + step)
            if len(self.results) >= window:
                values, self.results[-window] = lax.optimization_barrier((values, self.results[-window]))
            pairs = [(i, i ^ k) for i in range(self.parts)]
            places[k] = len(self.results)
            self.results.append(lax.ppermute(values, "seq", pairs))
        return ((pieces[0], places), *hooked) if hooks else (pieces[0], places)

    def get(self, sent):
        own, places = sent
        return [own] + [self.results[places[k]] for k in range(1, self.parts)]


def on_device(inputs, cotangent, kernel, factor_one, factor_two):
    batch_count, row_count, channels = inputs.shape
    block_size = factor_one.shape[0]
    block_count = factor_two.shape[0]
    local_blocks = row_count // block_size
    parts = lax.axis_size("seq")
    own = channels // parts
    group = min(LANES, channels) // own
    me = lax.axis_index("seq")
    me_array = me.reshape(1).astype(jnp.int32)
    send = Sends(parts)

    def pack(values, place):
        cube = values.reshape(-1, local_blocks, block_size, channels)
        pieces = []
        for lane_block in range(parts // group):
            pieces += leave(cube, place, me_array, lane_block, group)
        return pieces

    def unpack(pieces, place, count, onto):
        for lane_block in range(parts // group):
            some = pieces[lane_block * group : (lane_block + 1) * group]
            onto = arrive(some, me_array, lane_block, place, count, channels, onto)
        return onto

    def relative(values, axis):
        starts = [(me ^ k) * local_blocks for k in range(parts)]
        return jnp.concatenate([lax.dynamic_slice_in_dim(values, s, local_blocks, axis) for s in starts], axis)

    two = relative(relative(factor_two, 0), 1)
    factors = (factor_one, factor_one.T, two, two.T)
    kernel_sent = send(pack(kernel, 0))
    batch_sent = [(send(pack(inputs, n)), send(pack(cotangent, n))) for n in range(batch_count)]
    k_all = send.get(kernel_sent)
    grads_sent = []
    previous = None
    first_sum = second_sum = 0.0
    for n, (x_sent, y_sent) in enumerate(batch_sent):
        is_last = n == batch_count - 1
        grads, kernel_grads, first, second = mix(send.get(x_sent), send.get(y_sent), k_all, previous, is_last, factors)
        previous = kernel_grads[0]
        first_sum, second_sum = first_sum + first, second_sum + second
        if not is_last:
            grads_sent.append(send(grads))

    axes = ("dp", "seq")
    devices = lax.axis_size(axes)

    def reduced():
        both = jnp.concatenate([first_sum, relative(relative(second_sum, 0), 1)])
        shares = both.reshape(devices, -1, both.shape[1])
        return jnp.sum(lax.all_to_all(shares, axes, 0, 0, tiled=True), axis=0)

    def early_grads():
        done = None
        for n, sent in enumerate(grads_sent):
            done = unpack(send.get(sent), n, batch_count, done)
        return done

    kernel_sent = send(kernel_grads, first_window=2)
    steps = parts - 1
    last_sent, share, grad_inputs, grad_kernel = send(
        grads,
        (
            (0, reduced),
            (steps // 2, early_grads),
            (steps - 1, lambda: unpack(send.get(kernel_sent), 0, 1, None)),
        ),
    )
    last = send.get(last_sent)
    share, last[-1] = lax.optimization_barrier((share, last[-1]))
    copies = jnp.broadcast_to(share, (devices, *share.shape))
    totals = lax.all_to_all(copies, axes, 0, 0, tiled=True).reshape(-1, block_size)
    first_total, second_total = totals[:block_size], totals[block_size:]
    grad_inputs = unpack(last, batch_count - 1, batch_count, grad_inputs)
    full_width = channels * lax.axis_size("dp")
    scale_first = 1.0 / math.sqrt(batch_count * block_count * full_width)
    scale_second = 1.0 / math.sqrt(batch_count * block_size * full_width)
    return (
        grad_inputs.reshape(inputs.shape),
        grad_kernel.reshape(kernel.shape),
        first_total * scale_first,
        second_total * scale_second,
    )


def solution(mesh):
    return jax.shard_map(
        on_device,
        mesh=mesh,
        in_specs=(P(None, "seq", "dp"), P(None, "seq", "dp"), P("seq", "dp"), P(), P()),
        out_specs=(P(None, "seq", "dp"), P("seq", "dp"), P(), P()),
        check_vma=False,
    )
```

```python
import functools
import math

import jax
import jax.numpy as jnp
from jax import lax
from jax.experimental import pallas as pl
from jax.experimental.pallas import tpu as pltpu
from jax.sharding import PartitionSpec as P

WINDOW = 6
VMEM_BYTES = 60 * 1024 * 1024
LANES = 128
ROWS = 16


def matmul(left, right):
    return jnp.dot(left, right, preferred_element_type=jnp.float32)


def matmul_rows(left, right):
    return lax.dot_general(left, right, (((0,), (0,)), ((), ())), preferred_element_type=jnp.float32)


def matmul_columns(left, right):
    return lax.dot_general(left, right, (((1,), (1,)), ((), ())), preferred_element_type=jnp.float32)


def leave_kernel(group, me_ref, values_ref, *refs):
    outs, held = refs[:-1], refs[-1]
    mine = lax.rem(me_ref[0], group)
    turned = jnp.stack([values_ref[0, i].T for i in range(values_ref.shape[1])])
    held[...] = jnp.swapaxes(turned, 0, 1).reshape(held.shape)
    for j, out in enumerate(outs):
        out[...] = held[mine ^ j]


def leave(values, place, me, lane_block, group):
    _, blocks, width, channels = values.shape
    lanes = min(LANES, channels)
    own = lanes // group
    rows = math.gcd(blocks, ROWS)
    spec = pl.BlockSpec((own, rows, width), lambda i, me: (0, i, 0))
    return pl.pallas_call(
        functools.partial(leave_kernel, group),
        grid_spec=pltpu.PrefetchScalarGridSpec(
            num_scalar_prefetch=1,
            grid=(blocks // rows,),
            in_specs=[
                pl.BlockSpec((1, rows, width, lanes), lambda i, me: (place, i, 0, (me[0] // group) ^ lane_block))
            ],
            out_specs=[spec] * group,
            scratch_shapes=[pltpu.VMEM((group, own, rows, width), values.dtype)],
        ),
        out_shape=[jax.ShapeDtypeStruct((own, blocks, width), values.dtype)] * group,
        compiler_params=pltpu.CompilerParams(vmem_limit_bytes=VMEM_BYTES),
        cost_estimate=pl.CostEstimate(
            flops=0, bytes_accessed=4 * blocks * width * lanes, transcendentals=0
        ),
    )(me, values)


def arrive_kernel(group, me_ref, *refs):
    pieces, out_ref, held = refs[:group], refs[-2], refs[-1]
    own, blocks, width = pieces[0].shape
    mine = lax.rem(me_ref[0], group)
    for j, piece in enumerate(pieces):
        held[mine ^ j] = piece[...]
    turned = jnp.swapaxes(held[...].reshape(group * own, blocks, width), 0, 1)
    for i in range(blocks):
        out_ref[0, i] = turned[i].T


def arrive(pieces, me, lane_block, place, count, channels, onto):
    group = len(pieces)
    own, blocks, width = pieces[0].shape
    lanes = own * group
    rows = math.gcd(blocks, ROWS)
    spec = pl.BlockSpec((own, rows, width), lambda i, me: (0, i, 0))
    aliased = onto is not None
    return pl.pallas_call(
        functools.partial(arrive_kernel, group),
        grid_spec=pltpu.PrefetchScalarGridSpec(
            num_scalar_prefetch=1,
            grid=(blocks // rows,),
            in_specs=[spec] * group + ([pl.BlockSpec(memory_space=pl.ANY)] if aliased else []),
            out_specs=pl.BlockSpec(
                (1, rows, width, lanes), lambda i, me: (place, i, 0, (me[0] // group) ^ lane_block)
            ),
            scratch_shapes=[pltpu.VMEM((group, own, rows, width), pieces[0].dtype)],
        ),
        out_shape=jax.ShapeDtypeStruct((count, blocks, width, channels), pieces[0].dtype),
        input_output_aliases={group + 1: 0} if aliased else {},
        compiler_params=pltpu.CompilerParams(vmem_limit_bytes=VMEM_BYTES),
        cost_estimate=pl.CostEstimate(
            flops=0, bytes_accessed=4 * blocks * width * lanes, transcendentals=0
        ),
    )(me, *pieces, *((onto,) if aliased else ()))


def mix_kernel(parts, has_previous, is_last, *refs):
    refs = list(refs)
    take = lambda count: [refs.pop(0) for _ in range(count)]
    x_refs, y_refs, k_refs = take(parts), take(parts), take(parts)
    previous_ref = take(1)[0] if has_previous else None
    one_ref, one_t_ref, two_ref, two_t_ref = take(4)
    grad_refs = take(parts)
    kernel_refs = take(parts if is_last else 1)
    first_ref, second_ref = refs
    channel_count, part_rows, width = x_refs[0].shape

    @pl.when(pl.program_id(0) == 0)
    def _():
        first_ref[...] = jnp.zeros_like(first_ref)
        second_ref[...] = jnp.zeros_like(second_ref)

    def whole(group, channel):
        return jnp.concatenate([r[channel] for r in group], axis=0)

    def spread(group, channel, values):
        for part, ref in enumerate(group):
            ref[channel] = values[part * part_rows : (part + 1) * part_rows]

    one, one_t, two, two_t = one_ref[...], one_t_ref[...], two_ref[...], two_t_ref[...]
    first_sum = None
    second_sum = None
    for channel in range(channel_count):
        x, y = whole(x_refs, channel), whole(y_refs, channel)
        k = whole(k_refs, channel).astype(jnp.float32)
        a = matmul(x, one_t).astype(jnp.bfloat16)
        g = matmul(y, one_t).astype(jnp.bfloat16)
        s = matmul(two, a).astype(jnp.bfloat16).astype(jnp.float32)
        h = matmul(two, g).astype(jnp.bfloat16).astype(jnp.float32)
        z = (k * s).astype(jnp.bfloat16)
        w = (k * h).astype(jnp.bfloat16)
        kernel_terms = s * h
        if has_previous:
            kernel_terms = kernel_terms + previous_ref[channel]
        if is_last:
            spread(kernel_refs, channel, kernel_terms.astype(jnp.bfloat16))
        else:
            kernel_refs[0][channel] = kernel_terms
        c = matmul(two_t, z).astype(jnp.bfloat16)
        v = matmul(two_t, w).astype(jnp.bfloat16)
        spread(grad_refs, channel, matmul(v, one).astype(jnp.bfloat16))
        first = matmul_rows(c, y) + matmul_rows(v, x)
        second = matmul_columns(z, g) + matmul_columns(w, a)
        first_sum = first if first_sum is None else first_sum + first
        second_sum = second if second_sum is None else second_sum + second
    first_ref[...] += first_sum
    second_ref[...] += second_sum


def mix(x, y, k, previous, is_last, factors):
    parts = len(k)
    channels, part_rows, width = k[0].shape
    rows = parts * part_rows
    step = math.gcd(channels, 4)
    block = pl.BlockSpec((step, part_rows, width), lambda i: (i, 0, 0))
    tall = pl.BlockSpec((step, rows, width), lambda i: (i, 0, 0))
    has_previous = previous is not None
    small = [pl.BlockSpec(f.shape, lambda i: (0, 0)) for f in factors]
    sums = [jax.ShapeDtypeStruct((width, width), jnp.float32), jax.ShapeDtypeStruct((rows, rows), jnp.float32)]
    piece = jax.ShapeDtypeStruct((channels, part_rows, width), jnp.bfloat16)
    partial = jax.ShapeDtypeStruct((channels, rows, width), jnp.float32)
    out = pl.pallas_call(
        functools.partial(mix_kernel, parts, has_previous, is_last),
        grid=(channels // step,),
        in_specs=[block] * (3 * parts) + [tall] * has_previous + small,
        out_specs=[block] * parts
        + ([block] * parts if is_last else [tall])
        + [pl.BlockSpec(s.shape, lambda i: (0, 0)) for s in sums],
        out_shape=[piece] * parts + ([piece] * parts if is_last else [partial]) + sums,
        compiler_params=pltpu.CompilerParams(
            dimension_semantics=("arbitrary",), vmem_limit_bytes=VMEM_BYTES
        ),
        cost_estimate=pl.CostEstimate(
            flops=22 * channels * rows * width * width,
            bytes_accessed=12 * channels * rows * width,
            transcendentals=0,
        ),
    )(*x, *y, *k, *((previous,) if has_previous else ()), *factors)
    return out[:parts], out[parts:-2], out[-2], out[-1]


class Sends:
    def __init__(self, parts):
        self.parts = parts
        self.results = []

    def order(self):
        half = self.parts // 2
        far, near = list(range(half, self.parts)), list(range(1, half))
        mixed = []
        while far or near:
            mixed += [q.pop(0) for q in (far, near) if q]
        return mixed

    def __call__(self, pieces, hooks=(), first_window=WINDOW):
        places = {}
        hooked = []
        for step, k in enumerate(self.order()):
            values = pieces[k]
            for at, make in hooks:
                if at == step:
                    values, made = lax.optimization_barrier((values, make()))
                    hooked.append(made)
            window = min(WINDOW, first_window + step)
            if len(self.results) >= window:
                values, self.results[-window] = lax.optimization_barrier((values, self.results[-window]))
            pairs = [(i, i ^ k) for i in range(self.parts)]
            places[k] = len(self.results)
            self.results.append(lax.ppermute(values, "seq", pairs))
        return ((pieces[0], places), *hooked) if hooks else (pieces[0], places)

    def get(self, sent):
        own, places = sent
        return [own] + [self.results[places[k]] for k in range(1, self.parts)]


def on_device(inputs, cotangent, kernel, factor_one, factor_two):
    batch_count, row_count, channels = inputs.shape
    block_size = factor_one.shape[0]
    block_count = factor_two.shape[0]
    local_blocks = row_count // block_size
    parts = lax.axis_size("seq")
    own = channels // parts
    group = min(LANES, channels) // own
    me = lax.axis_index("seq")
    me_array = me.reshape(1).astype(jnp.int32)
    send = Sends(parts)

    def pack(values, place):
        cube = values.reshape(-1, local_blocks, block_size, channels)
        pieces = []
        for lane_block in range(parts // group):
            pieces += leave(cube, place, me_array, lane_block, group)
        return pieces

    def unpack(pieces, place, count, onto):
        for lane_block in range(parts // group):
            some = pieces[lane_block * group : (lane_block + 1) * group]
            onto = arrive(some, me_array, lane_block, place, count, channels, onto)
        return onto

    def relative(values, axis):
        starts = [(me ^ k) * local_blocks for k in range(parts)]
        return jnp.concatenate([lax.dynamic_slice_in_dim(values, s, local_blocks, axis) for s in starts], axis)

    two = relative(relative(factor_two, 0), 1)
    factors = (factor_one, factor_one.T, two, two.T)
    kernel_sent = send(pack(kernel, 0))
    batch_sent = [(send(pack(inputs, n)), send(pack(cotangent, n))) for n in range(batch_count)]
    k_all = send.get(kernel_sent)
    grads_sent = []
    previous = None
    first_sum = second_sum = 0.0
    for n, (x_sent, y_sent) in enumerate(batch_sent):
        is_last = n == batch_count - 1
        grads, kernel_grads, first, second = mix(send.get(x_sent), send.get(y_sent), k_all, previous, is_last, factors)
        previous = kernel_grads[0]
        first_sum, second_sum = first_sum + first, second_sum + second
        if not is_last:
            grads_sent.append(send(grads))

    axes = ("dp", "seq")
    devices = lax.axis_size(axes)

    def reduced():
        both = jnp.concatenate([first_sum, relative(relative(second_sum, 0), 1)])
        for axis in axes:
            shares = both.reshape(lax.axis_size(axis), -1, both.shape[1])
            both = jnp.sum(lax.all_to_all(shares, axis, 0, 0, tiled=True), axis=0)
        return both

    def early_grads():
        done = None
        for n, sent in enumerate(grads_sent):
            done = unpack(send.get(sent), n, batch_count, done)
        return done

    kernel_sent = send(kernel_grads, first_window=2)
    steps = parts - 1
    last_sent, share, grad_inputs, grad_kernel = send(
        grads,
        (
            (0, reduced),
            (steps // 2, early_grads),
            (steps - 1, lambda: unpack(send.get(kernel_sent), 0, 1, None)),
        ),
    )
    last = send.get(last_sent)
    share, last[-1] = lax.optimization_barrier((share, last[-1]))
    copies = jnp.broadcast_to(share, (devices, *share.shape))
    totals = lax.all_to_all(copies, axes, 0, 0, tiled=True).reshape(-1, block_size)
    first_total, second_total = totals[:block_size], totals[block_size:]
    grad_inputs = unpack(last, batch_count - 1, batch_count, grad_inputs)
    full_width = channels * lax.axis_size("dp")
    scale_first = 1.0 / math.sqrt(batch_count * block_count * full_width)
    scale_second = 1.0 / math.sqrt(batch_count * block_size * full_width)
    return (
        grad_inputs.reshape(inputs.shape),
        grad_kernel.reshape(kernel.shape),
        first_total * scale_first,
        second_total * scale_second,
    )


def solution(mesh):
    return jax.shard_map(
        on_device,
        mesh=mesh,
        in_specs=(P(None, "seq", "dp"), P(None, "seq", "dp"), P("seq", "dp"), P(), P()),
        out_specs=(P(None, "seq", "dp"), P("seq", "dp"), P(), P()),
        check_vma=False,
    )
```
